128 devices in a mesh: seq: 8 (over x, y_lo), fsdp: 16 (over z, y_hi, core).
Axes of the slice: x: 4, y: 4 (y_hi: 2, y_lo: 2; y = y_hi * 2 + y_lo), z: 4, core: 2. Of those that a mesh axis runs over, the one named last changes fastest.
Arguments:
- tokens: bfloat16 [16, 1024, 1152], P('fsdp', 'seq'), may hold values from -6 to 6
- w_attn: bfloat16 [1152, 2560], P('fsdp'), may hold values from -0.1875 to 0.1875
- w_mlp: bfloat16 [1152, 20736], P('fsdp'), may hold values from -0.1875 to 0.1875
- norm_gains: bfloat16 [4, 1152], P(None, 'fsdp'), may hold values from 0.25 to 1.75
- qk_gains: bfloat16 [2, 256], P(None, 'fsdp'), may hold values from 0.25 to 1.75
- cotangent: bfloat16 [16, 1024, 1152], P('fsdp', 'seq'), may hold values from -6 to 6
Outputs:
- result: bfloat16 [16, 1024, 1152], P('fsdp', 'seq')
- tokens_grad: float32 [16, 1024, 1152], P('fsdp', 'seq')
- w_attn_grad: float32 [1152, 2560], P('fsdp')
- w_mlp_grad: float32 [1152, 20736], P('fsdp')
- norm_gains_grad: float32 [4, 1152], P(None, 'fsdp')
- qk_gains_grad: float32 [2, 256], P(None, 'fsdp')
The draws below stay inside these ranges and needn't reach their ends.
All inputs are finite; a program needn't handle non-finite values.
Results may differ from the reference program's by a relative error of at most 0.025.
Values may be sent and summed in bfloat16 or wider, within the bound.
A program may use at most 320 MiB of HBM per device.

```python
from functools import partial
import jax
import jax.numpy as jnp
from jax import lax

D = 1152
HEADS = 4
HEAD = 256
FF = 6912
WINDOW = 512
LENGTH = 1024
SEQS = 16


def block_scale(own_key, extent, cuts, least, top_value):
    gain = 1.0
    for position, parts in cuts:
        steps = jax.random.uniform(jax.random.fold_in(jax.random.fold_in(own_key, 6), position), (parts,), jnp.float32, least / len(cuts), top_value / len(cuts))
        gain = gain * jnp.repeat(jnp.exp(steps), extent[position] // parts).reshape((-1,) + (1,) * (len(extent) - 1 - position))
    return gain


def normal_values(rng, shape, scale, reach, cuts=(), held_as=jnp.bfloat16):
    drawn = scale * jax.random.normal(rng, shape, jnp.float32)
    if cuts:
        drawn = drawn * block_scale(rng, shape, cuts, -0.22, 0.18)
    return jnp.clip(drawn, -reach, reach).astype(held_as)


def setup_inputs(seed: int = 0) -> dict:
    seeds = jax.random.split(jax.random.key(seed), 7)
    tokens = normal_values(seeds[0], (SEQS, LENGTH, D), 1.0, 6.0, ((0, 16), (1, 8)))
    w_attn = normal_values(seeds[1], (D, (2 * HEADS + 2) * HEAD), D ** -0.5, 0.1875, ((0, 16),))
    w_mlp = normal_values(seeds[2], (D, 3 * FF), D ** -0.5, 0.1875, ((0, 16),))
    norm_gains = jnp.clip(1.0 + 0.15 * jax.random.normal(seeds[3], (4, D), jnp.float32), 0.25, 1.75).astype(jnp.bfloat16)
    qk_gains = jnp.clip(1.0 + 0.15 * jax.random.normal(seeds[4], (2, HEAD), jnp.float32), 0.25, 1.75).astype(jnp.bfloat16)
    cotangent = normal_values(seeds[5], (SEQS, LENGTH, D), 1.0, 6.0, ((0, 16), (1, 8)))
    return {"tokens": tokens, "w_attn": w_attn, "w_mlp": w_mlp, "norm_gains": norm_gains, "qk_gains": qk_gains, "cotangent": cotangent}


@jax.custom_vjp
def low(v):
    return lax.optimization_barrier(v.astype(jnp.bfloat16)).astype(jnp.float32)

@jax.custom_vjp
def low_back(v):
    return v

def low_keep(v):
    return (low(v), None)

def low_pass(kept, grad):
    return (grad,)

def back_keep(v):
    return (v, None)

def back_low(kept, grad):
    return (low(grad),)
low.defvjp(low_keep, low_pass)
low_back.defvjp(back_keep, back_low)
EPSILON = 1e-06
ROPE_BASE = 10000.0
MASKED = -1e+30

def rms_norm(values, scale):
    return values * lax.rsqrt(lax.optimization_barrier(jnp.mean(values * values, axis=-1, keepdims=True)) + EPSILON) * scale

def rotate(values, cos_part, sin_part):
    half_size = values.shape[-1] // 2
    turned = jnp.concatenate([-values[..., half_size:], values[..., :half_size]], axis=-1)
    return values * cos_part + turned * sin_part

def tables(positions):
    half_size = HEAD // 2
    frequency = ROPE_BASE ** (-(jnp.arange(half_size, dtype=jnp.float32) * 2.0) / HEAD)
    angles = positions[:, None] * frequency[None, :]
    cos_table = jnp.concatenate([jnp.cos(angles), jnp.cos(angles)], axis=-1)
    sin_table = jnp.concatenate([jnp.sin(angles), jnp.sin(angles)], axis=-1)
    return (cos_table, sin_table)

def window_block(queries, key_rows, value_rows, first_row):
    scores = low_back(jnp.einsum('whc,tc->hwt', queries, key_rows, precision=lax.Precision.HIGHEST))
    row_index = first_row + jnp.arange(WINDOW, dtype=jnp.int32)
    col_index = first_row - WINDOW + jnp.arange(2 * WINDOW, dtype=jnp.int32)
    distance = row_index[:, None] - col_index[None, :]
    allowed = (distance >= 0) & (distance < WINDOW) & (col_index[None, :] >= 0)
    scores = jnp.where(allowed[None], scores, MASKED)
    weights = low(jax.nn.softmax(scores, axis=-1))
    return jnp.einsum('hwt,tc->whc', weights, value_rows, precision=lax.Precision.HIGHEST)

def attend(queries, key_rows, value_rows):
    block_count = LENGTH // WINDOW
    query_blocks = queries.reshape(block_count, WINDOW, HEADS, HEAD)
    padding = jnp.zeros((WINDOW, HEAD), jnp.float32)
    key_stack = jnp.concatenate([padding, key_rows], axis=0).reshape(block_count + 1, WINDOW, HEAD)
    value_stack = jnp.concatenate([padding, value_rows], axis=0).reshape(block_count + 1, WINDOW, HEAD)
    key_blocks = jnp.concatenate([key_stack[:-1], key_stack[1:]], axis=1)
    value_blocks = jnp.concatenate([value_stack[:-1], value_stack[1:]], axis=1)
    firsts = jnp.arange(block_count, dtype=jnp.int32) * WINDOW
    checked = jax.checkpoint(window_block)
    mixed = lax.map(lambda packed: checked(packed[0], packed[1], packed[2], packed[3]), (query_blocks, key_blocks, value_blocks, firsts))
    return mixed.reshape(LENGTH, HEADS * HEAD)

def forward_layer(inputs, w_attn, w_mlp, norm_gains, qk_gains, cos_table, sin_table):
    q_width = HEADS * HEAD
    split_qkv = q_width + 2 * HEAD
    hidden_in = low(rms_norm(inputs, norm_gains[0]))
    project = low_back(jnp.dot(hidden_in, w_attn[:, :split_qkv], precision=lax.Precision.HIGHEST))
    queries = project[:, :q_width].reshape(LENGTH, HEADS, HEAD)
    key_rows = project[:, q_width:q_width + HEAD]
    value_rows = low(project[:, q_width + HEAD:])
    queries = rotate(rms_norm(queries, qk_gains[0]), cos_table[:, None, :], sin_table[:, None, :])
    queries = low(low_back(queries * HEAD ** (-0.5)))
    key_rows = low(low_back(rotate(rms_norm(key_rows, qk_gains[1]), cos_table, sin_table)))
    mixed = low(low_back(attend(queries, key_rows, value_rows)))
    branch = low_back(jnp.dot(mixed, w_attn[:, split_qkv:].T, precision=lax.Precision.HIGHEST))
    middle = inputs + rms_norm(branch, norm_gains[1])
    hidden_ff = low(rms_norm(middle, norm_gains[2]))
    gate_up = low_back(jnp.dot(hidden_ff, w_mlp[:, :2 * FF], precision=lax.Precision.HIGHEST))
    product = low(jax.nn.gelu(gate_up[:, :FF], approximate=True) * gate_up[:, FF:])
    branch_ff = low_back(jnp.dot(product, w_mlp[:, 2 * FF:].T, precision=lax.Precision.HIGHEST))
    return middle + rms_norm(branch_ff, norm_gains[3])

def reference(tokens, w_attn, w_mlp, norm_gains, qk_gains, cotangent):
    attn_f = w_attn.astype(jnp.float32)
    mlp_f = w_mlp.astype(jnp.float32)
    gains_f = norm_gains.astype(jnp.float32)
    qk_f = qk_gains.astype(jnp.float32)
    cos_table, sin_table = tables(jnp.arange(LENGTH, dtype=jnp.float32))
    layer_fn = partial(forward_layer, cos_table=cos_table, sin_table=sin_table)

    def one_sequence(running, paired):
        row_in, row_grad = paired
        output, pullback = jax.vjp(layer_fn, row_in.astype(jnp.float32), attn_f, mlp_f, gains_f, qk_f)
        gradients = pullback(row_grad.astype(jnp.float32))
        running = tuple((before + gradient for before, gradient in zip(running, gradients[1:])))
        return (running, (output.astype(jnp.bfloat16), gradients[0]))
    initial = (jnp.zeros_like(attn_f), jnp.zeros_like(mlp_f), jnp.zeros_like(gains_f), jnp.zeros_like(qk_f))
    running, (outputs, input_grads) = lax.scan(one_sequence, initial, (tokens, cotangent))
    return (outputs, input_grads, running[0], running[1], running[2], running[3])
```

```python
from functools import partial

import jax
import jax.numpy as jnp
from jax import lax
from jax.experimental import pallas as pl
from jax.experimental.pallas import tpu as pltpu
from jax.sharding import Mesh
from jax.sharding import PartitionSpec as P

HEADS = 4
HEAD = 256
FF = 6912
WINDOW = 512


EPSILON = 1e-06
ROPE_BASE = 10000.0
MASKED = -1e30


def inverse_rms(values):
    return lax.rsqrt(jnp.mean(values * values, axis=-1, keepdims=True) + EPSILON)


MESH = pl.DeviceIdType.MESH
LANES = 128
ROWS = 128
CHIPS = 4


def vmem_spec():
    return pl.BlockSpec(memory_space=pltpu.VMEM)


def nt_dot(left, right):
    return lax.dot_general(
        left, right, (((1,), (1,)), ((), ())), preferred_element_type=jnp.float32
    )


def meet(peers):
    barrier = pltpu.get_barrier_semaphore()
    for peer in peers:
        pl.semaphore_signal(barrier, inc=1, device_id=peer, device_id_type=MESH)
    pl.semaphore_wait(barrier, len(peers))


def group_peers():
    chip, core = lax.axis_index("x"), lax.axis_index("c")
    sibling = {"c": 1 - core}
    right = {"x": lax.rem(chip + 1, CHIPS)}
    left = {"x": lax.rem(chip + CHIPS - 1, CHIPS)}
    return sibling, right, left


def rows_of(chip_step, core_step, first=0, count=ROWS):
    return pl.ds((chip_step * 2 + core_step) * ROWS + first, count)


def exchange_stage(blocks, partial, sib_in, outgoing, inbox, transit, sends, recvs, chunk, filler):
    sibling, right, left = group_peers()
    half = ROWS // 2

    def copy(number, source, target, peer):
        return pltpu.make_async_remote_copy(
            src_ref=source,
            dst_ref=target,
            send_sem=sends.at[number],
            recv_sem=recvs.at[number],
            device_id=peer,
            device_id_type=MESH,
        )

    own = blocks.at[rows_of(0, 0)]
    started = []

    def start(*args):
        made = copy(*args)
        made.start()
        started.append(made)
        return made

    to_right = start(0, own, blocks.at[rows_of(3, 0)], right)
    to_left = start(1, own, blocks.at[rows_of(1, 0)], left)
    to_sib = start(2, own, blocks.at[rows_of(0, 1)], sibling)

    def run(step):
        partial[pl.ds(step * 2 * ROWS, 2 * ROWS), :] = chunk(step)
        outgoing[rows_of(step, 1), :] = partial[rows_of(step, 1), :].astype(jnp.bfloat16)
        return start(
            8 + step, outgoing.at[rows_of(step, 1)], sib_in.at[pl.ds(step * ROWS, ROWS)], sibling
        )

    def paired(step, given):
        given.wait_recv()
        both = partial[rows_of(step, 0), :] + sib_in[pl.ds(step * ROWS, ROWS), :].astype(
            jnp.float32
        )
        outgoing[rows_of(step, 0), :] = both.astype(jnp.bfloat16)

    to_sib.wait_recv()
    sib_0 = run(0)
    to_right.wait_recv()
    share_3 = start(3, blocks.at[rows_of(3, 0)], blocks.at[rows_of(3, 1)], sibling)
    far_right = start(
        4, blocks.at[rows_of(3, 0, 0, half)], blocks.at[rows_of(2, 0, 0, half)], right
    )
    to_left.wait_recv()
    share_1 = start(5, blocks.at[rows_of(1, 0)], blocks.at[rows_of(1, 1)], sibling)
    far_left = start(
        6, blocks.at[rows_of(1, 0, half, half)], blocks.at[rows_of(2, 0, half, half)], left
    )
    share_3.wait_recv()
    sib_3 = run(3)
    far_right.wait_recv()
    far_left.wait_recv()
    share_2 = start(7, blocks.at[rows_of(2, 0)], blocks.at[rows_of(2, 1)], sibling)
    paired(3, sib_3)
    sum_left = start(12, outgoing.at[rows_of(3, 0)], inbox.at[pl.ds(ROWS, ROWS)], left)
    share_1.wait_recv()
    sib_1 = run(1)
    share_2.wait_recv()
    paired(1, sib_1)
    sum_right = start(13, outgoing.at[rows_of(1, 0)], inbox.at[pl.ds(3 * ROWS, ROWS)], right)
    sib_2 = run(2)
    paired(2, sib_2)
    hop_right = start(14, outgoing.at[rows_of(2, 0, 0, half)], transit.at[pl.ds(0, half)], right)
    hop_left = start(15, outgoing.at[rows_of(2, 0, half, half)], transit.at[pl.ds(half, half)], left)
    filler(0)
    hop_right.wait_recv()
    on_right = start(
        16, transit.at[pl.ds(0, half)], inbox.at[pl.ds(2 * ROWS, half)], right
    )
    hop_left.wait_recv()
    on_left = start(
        17, transit.at[pl.ds(half, half)], inbox.at[pl.ds(2 * ROWS + half, half)], left
    )
    filler(1)
    sib_0.wait_recv()
    sum_left.wait_recv()
    sum_right.wait_recv()
    total = partial[rows_of(0, 0), :] + sib_in[pl.ds(0, ROWS), :].astype(jnp.float32)
    total += inbox[pl.ds(ROWS, ROWS), :].astype(jnp.float32)
    total += inbox[pl.ds(3 * ROWS, ROWS), :].astype(jnp.float32)
    on_right.wait_recv()
    on_left.wait_recv()
    total += inbox[pl.ds(2 * ROWS, ROWS), :].astype(jnp.float32)
    for made in started:
        made.wait_send()
    return total


def mlp_kernel(
    hidden_ref,
    middle_ref,
    cot_ref,
    weights_ref,
    gain_ref,
    result_ref,
    grad_hidden_ref,
    gain_grad_ref,
    dw_gu_ref,
    dw_d_ref,
    hidden_all,
    down_all,
    product_all,
    gu_all,
    kept_a,
    kept_b,
    partial,
    sib_in,
    outgoing,
    inbox,
    transit,
    sends,
    recvs,
):
    width = weights_ref.shape[1] // 3
    tiles = width // LANES
    wgu_ref = weights_ref.at[:, pl.ds(0, 2 * width)]
    wd_ref = weights_ref.at[:, pl.ds(2 * width, width)]
    meet(group_peers())
    hidden_all[rows_of(0, 0), :] = hidden_ref[...]
    gelu_scale = 0.7978845608028654

    def forward_chunk(step):
        first = step * 2 * ROWS
        rows = pl.ds(first, 2 * ROWS)

        def tile(index, carry):
            at = pl.multiple_of(index * LANES, LANES)
            both = jnp.dot(
                hidden_all[rows, :],
                wgu_ref[:, pl.ds(pl.multiple_of(2 * at, 2 * LANES), 2 * LANES)],
                preferred_element_type=jnp.float32,
            )
            gate, up = both[:, :LANES], both[:, LANES:]
            square = gate * gate
            turned = jnp.tanh(gelu_scale * gate * (1.0 + 0.044715 * square))
            halved = 0.5 * (1.0 + turned)
            gelu = gate * halved
            slope = halved + 0.5 * gate * (1.0 - turned * turned) * gelu_scale * (
                1.0 + 3 * 0.044715 * square
            )
            product_all[rows, pl.ds(at, LANES)] = (gelu * up).astype(jnp.bfloat16)
            kept_a[rows, pl.ds(at, LANES)] = gelu
            kept_b[rows, pl.ds(at, LANES)] = up * slope
            return carry

        lax.fori_loop(0, tiles, tile, 0)
        return nt_dot(product_all[rows, :], wd_ref[...])

    branch = exchange_stage(
        hidden_all, partial, sib_in.at[0], outgoing.at[0], inbox.at[0], transit.at[0],
        sends.at[0], recvs.at[0], forward_chunk, lambda place: None,
    )
    gain = gain_ref[...]
    grad_out = cot_ref[...].astype(jnp.float32)
    inverse = lax.rsqrt(jnp.mean(branch * branch, axis=-1, keepdims=True) + EPSILON)
    normed = branch * inverse
    result_ref[...] = (middle_ref[...] + normed * gain).astype(jnp.bfloat16)
    gain_grad_ref[...] = jnp.sum(grad_out * normed, axis=0, keepdims=True)
    scaled = grad_out * gain
    down_all[rows_of(0, 0), :] = (
        inverse * (scaled - normed * jnp.mean(scaled * normed, axis=-1, keepdims=True))
    ).astype(jnp.bfloat16)

    def backward_chunk(step):
        first = step * 2 * ROWS
        rows = pl.ds(first, 2 * ROWS)

        for first_tile in range(0, tiles, 2):
            at = first_tile * LANES
            size = min(2 * LANES, width - at)
            grad = jnp.dot(
                down_all[rows, :], wd_ref[:, at : at + size], preferred_element_type=jnp.float32
            )
            gate_grad = low_of(grad * kept_b[rows, at : at + size])
            up_grad = low_of(grad * kept_a[rows, at : at + size])
            for piece in range(0, size, LANES):
                here = 2 * (at + piece)
                gu_all[rows, here : here + LANES] = gate_grad[:, piece : piece + LANES]
                gu_all[rows, here + LANES : here + 2 * LANES] = up_grad[:, piece : piece + LANES]
        return nt_dot(gu_all[rows, :], wgu_ref[...])

    def weight_grads(place):
        if place == 1:
            turned = hidden_all[...].T
            for at in range(0, 2 * width, 256):
                dw_gu_ref[:, at : at + 256] = jnp.dot(
                    turned, gu_all[:, at : at + 256], preferred_element_type=jnp.float32
                ).astype(jnp.bfloat16)
        else:
            turned = down_all[...].T
            for at in range(0, width, 256):
                end = min(at + 256, width)
                dw_d_ref[:, at:end] = jnp.dot(
                    turned, product_all[:, at:end], preferred_element_type=jnp.float32
                ).astype(jnp.bfloat16)

    grad_hidden_ref[...] = exchange_stage(
        down_all, partial, sib_in.at[1], outgoing.at[1], inbox.at[1], transit.at[1],
        sends.at[1], recvs.at[1], backward_chunk, weight_grads,
    )


def mlp_call(hidden, middle, cot, weights, gain):
    rows, model_width = hidden.shape
    width = weights.shape[1] // 3
    group_rows = 2 * CHIPS * rows
    return pl.pallas_call(
        mlp_kernel,
        out_shape=(
            jax.ShapeDtypeStruct((rows, model_width), jnp.bfloat16),
            jax.ShapeDtypeStruct((rows, model_width), jnp.float32),
            jax.ShapeDtypeStruct((1, model_width), jnp.float32),
            jax.ShapeDtypeStruct((model_width, 2 * width), jnp.bfloat16),
            jax.ShapeDtypeStruct((model_width, width), jnp.bfloat16),
        ),
        in_specs=[vmem_spec()] * 5,
        out_specs=tuple([vmem_spec()] * 5),
        scratch_shapes=[
            pltpu.VMEM((group_rows, model_width), jnp.bfloat16),
            pltpu.VMEM((group_rows, model_width), jnp.bfloat16),
            pltpu.VMEM((group_rows, width), jnp.bfloat16),
            pltpu.VMEM((group_rows, 2 * width), jnp.bfloat16),
            pltpu.VMEM((group_rows, width), jnp.float32),
            pltpu.VMEM((group_rows, width), jnp.float32),
            pltpu.VMEM((group_rows, model_width), jnp.float32),
            pltpu.VMEM((2, CHIPS * rows, model_width), jnp.bfloat16),
            pltpu.VMEM((2, group_rows, model_width), jnp.bfloat16),
            pltpu.VMEM((2, CHIPS * rows, model_width), jnp.bfloat16),
            pltpu.VMEM((2, rows, model_width), jnp.bfloat16),
            pltpu.SemaphoreType.DMA((2, 18)),
            pltpu.SemaphoreType.DMA((2, 18)),
        ],
        compiler_params=pltpu.CompilerParams(
            collective_id=0, has_side_effects=True, vmem_limit_bytes=60 * 1024 * 1024
        ),
        cost_estimate=pl.CostEstimate(
            flops=6 * group_rows * model_width * 3 * width, bytes_accessed=20_000_000, transcendentals=0
        ),
        name="feed_forward",
    )(hidden, middle, cot, weights, gain)


def ring_peers(axis):
    place = lax.axis_index(axis)
    return (
        {axis: lax.rem(place + 1, CHIPS)},
        {axis: lax.rem(place + CHIPS - 1, CHIPS)},
        {axis: lax.rem(place + 2, CHIPS)},
    )


def column_peers():
    half, low = lax.axis_index("h"), lax.axis_index("l")
    return ({"h": 1 - half, "l": 1 - low}, {"l": 1 - low}, {"h": 1 - half})


class Copies:
    def __init__(self, sends, recvs):
        self.sends, self.recvs, self.made = sends, recvs, []

    def start(self, source, target, peer):
        number = len(self.made)
        copy = pltpu.make_async_remote_copy(
            src_ref=source,
            dst_ref=target,
            send_sem=self.sends.at[number],
            recv_sem=self.recvs.at[number],
            device_id=peer,
            device_id_type=MESH,
        )
        copy.start()
        self.made.append(copy)
        return copy

    def finish(self):
        for copy in self.made:
            copy.wait_send()


def run_flows(flows):
    waiting = []
    for order, flow in enumerate(flows):
        waiting.append((next(flow), order, flow))
    while waiting:
        waiting.sort(key=lambda entry: entry[:2])
        _, order, flow = waiting.pop(0)
        try:
            waiting.append((next(flow), order, flow))
        except StopIteration:
            pass


def wide(values):
    return values.astype(jnp.float32)


def low_of(values):
    return values.astype(jnp.bfloat16)


def rms_back_of(grad, normed, inverse):
    return inverse * (grad - normed * jnp.mean(grad * normed, axis=-1, keepdims=True))


def turn(values, cos_ref, sin_ref):
    half = HEAD // 2
    first, second = values[:, :half], values[:, half:]
    cos_part, sin_part = cos_ref[...], sin_ref[...]
    return jnp.concatenate(
        [first * cos_part - second * sin_part, second * cos_part + first * sin_part], axis=1
    )


def turn_back(grads, cos_ref, sin_ref):
    half = HEAD // 2
    first, second = grads[:, :half], grads[:, half:]
    cos_part, sin_part = cos_ref[...], sin_ref[...]
    return jnp.concatenate(
        [first * cos_part + second * sin_part, second * cos_part - first * sin_part], axis=1
    )


REACH = 4


def block_peer(step):
    block = lax.rem(lax.axis_index("x") * 2 + lax.axis_index("l") + step + 8, 8)
    return {"x": block // 2, "l": lax.rem(block, 2)}


def flat(values):
    return values.reshape(values.shape[0] * values.shape[1], values.shape[2])


def attention_flow(copies, times, weights, gains_of, tokens_ref, cos_ref, sin_ref, saved):
    gains_ref, qk_ref, raw, q_low, kv_all, probs, mixed, branch_ref, middle_ref, hidden_ref = saved
    seq_block = lax.axis_index("x") * 2 + lax.axis_index("l")
    rows = tokens_ref.shape[0]
    q_width = HEADS * HEAD
    yield times[0]
    gains_of()
    inputs = wide(tokens_ref[...])
    normed = inputs * inverse_rms(inputs)
    hidden_in = low_of(normed * gains_ref[0:1, :])
    for head in range(HEADS + 2):
        at = head * HEAD
        raw_part = jnp.dot(
            hidden_in, flat(weights[:, :, at : at + HEAD]), preferred_element_type=jnp.float32
        )
        if head <= HEADS:
            raw[:, at : at + HEAD] = raw_part
            which = 0 if head < HEADS else 1
            scaled = raw_part * inverse_rms(raw_part) * qk_ref[which : which + 1, :]
            turned = turn(scaled, cos_ref, sin_ref)
            if head < HEADS:
                q_low[:, at : at + HEAD] = low_of(turned * HEAD ** (-0.5))
            else:
                kv_all[REACH, :, :HEAD] = low_of(turned)
        else:
            kv_all[REACH, :, HEAD:] = low_of(raw_part)
    sent = [
        copies.start(kv_all.at[REACH], kv_all.at[REACH - step], block_peer(step))
        for step in range(1, REACH + 1)
    ]
    yield times[1]
    for copy in sent:
        copy.wait_recv()
    span = (REACH + 1) * rows
    row_pos = lax.broadcasted_iota(jnp.int32, (rows, span), 0)
    col_pos = lax.broadcasted_iota(jnp.int32, (rows, span), 1)
    distance = REACH * rows + row_pos - col_pos
    allowed = (
        (distance >= 0) & (distance < WINDOW) & ((seq_block - REACH) * rows + col_pos >= 0)
    )
    keys = flat(kv_all[:, :, :HEAD])
    values = flat(kv_all[:, :, HEAD:])
    for head in range(HEADS):
        at = head * HEAD
        scores = jnp.where(allowed, nt_dot(q_low[:, at : at + HEAD], keys), MASKED)
        exponent = jnp.exp(scores - jnp.max(scores, axis=-1, keepdims=True))
        share = exponent / jnp.sum(exponent, axis=-1, keepdims=True)
        probs[head] = share
        mixed[:, at : at + HEAD] = low_of(
            jnp.dot(low_of(share), values, preferred_element_type=jnp.float32)
        )
    yield times[2]
    branch = nt_dot(mixed[...], flat(weights[:, :, q_width + 2 * HEAD :]))
    branch_ref[...] = branch
    middle = wide(tokens_ref[...]) + branch * inverse_rms(branch) * gains_ref[1:2, :]
    middle_ref[...] = middle
    hidden_ref[...] = low_of(middle * inverse_rms(middle) * gains_ref[2:3, :])


def attention_back_flow(
    copies, times, grad_hidden_ref, po_ref, cot_ref, tokens_ref, weights, cos_ref, sin_ref, saved,
    dwa, small, grad_kv, kv_out, kv_in, grad_q, grad_middle_ref, proj, tokens_grad_ref,
):
    gains_ref, qk_ref, raw, q_low, kv_all, probs, mixed, branch_ref, middle_ref = saved
    q_width = HEADS * HEAD
    split_qkv = q_width + 2 * HEAD
    rows = tokens_ref.shape[0]
    tile = 256
    yield times[0]
    middle = middle_ref[...]
    inverse = inverse_rms(middle)
    normed = middle * inverse
    grad_hidden = grad_hidden_ref[...]
    small[...] = jnp.zeros_like(small)
    small[3:4, :] = po_ref[...]
    small[2:3, :] = jnp.sum(grad_hidden * normed, axis=0, keepdims=True)
    grad_middle = wide(cot_ref[...]) + rms_back_of(grad_hidden * gains_ref[2:3, :], normed, inverse)
    grad_middle_ref[...] = grad_middle
    branch = branch_ref[...]
    inverse = inverse_rms(branch)
    normed = branch * inverse
    small[1:2, :] = jnp.sum(grad_middle * normed, axis=0, keepdims=True)
    branch_low = low_of(rms_back_of(grad_middle * gains_ref[1:2, :], normed, inverse))
    turned = branch_low.T
    for at in range(0, q_width, tile):
        dwa[:, split_qkv + at : split_qkv + at + tile] = low_of(
            jnp.dot(turned, mixed[:, at : at + tile], preferred_element_type=jnp.float32)
        )
    yield times[1]
    grad_mixed = low_of(
        jnp.dot(branch_low, flat(weights[:, :, split_qkv:]), preferred_element_type=jnp.float32)
    )
    keys = flat(kv_all[:, :, :HEAD])
    values = flat(kv_all[:, :, HEAD:])
    for head in range(HEADS):
        at = head * HEAD
        grad_out = grad_mixed[:, at : at + HEAD]
        share = probs[head]
        grad_share = nt_dot(grad_out, values)
        delta = jnp.sum(share * grad_share, axis=-1, keepdims=True)
        score_grad = low_of(share * (grad_share - delta))
        grad_q[:, at : at + HEAD] = jnp.dot(score_grad, keys, preferred_element_type=jnp.float32)
        key_part = jnp.dot(
            score_grad.T, q_low[:, at : at + HEAD], preferred_element_type=jnp.float32
        )
        value_part = jnp.dot(low_of(share).T, grad_out, preferred_element_type=jnp.float32)
        if head == 0:
            grad_kv[:, :HEAD] = key_part
            grad_kv[:, HEAD:] = value_part
        else:
            grad_kv[:, :HEAD] += key_part
            grad_kv[:, HEAD:] += value_part
        if head == 1:
            yield times[2]
    kv_out[...] = low_of(grad_kv[: REACH * rows, :]).reshape(kv_out.shape)
    sent = [
        copies.start(kv_out.at[REACH - step], kv_in.at[REACH - step], block_peer(-step))
        for step in range(1, REACH + 1)
    ]
    yield times[3]
    for copy in sent:
        copy.wait_recv()
    grad_own = grad_kv[REACH * rows :, :]
    for step in range(REACH):
        grad_own += wide(kv_in[step])
    for head in range(HEADS + 1):
        at = head * HEAD
        which = 0 if head < HEADS else 1
        raw_part = raw[:, at : at + HEAD]
        inverse = inverse_rms(raw_part)
        normed = raw_part * inverse
        if head < HEADS:
            grad_turned = wide(low_of(grad_q[:, at : at + HEAD])) * HEAD ** (-0.5)
        else:
            grad_turned = wide(low_of(grad_own[:, :HEAD]))
        grad = turn_back(grad_turned, cos_ref, sin_ref)
        row = jnp.sum(grad * normed, axis=0, keepdims=True)
        small[4:5, which * HEAD : (which + 1) * HEAD] += row
        proj[:, at : at + HEAD] = low_of(
            rms_back_of(grad * qk_ref[which : which + 1, :], normed, inverse)
        )
    proj[:, q_width + HEAD :] = low_of(grad_own[:, HEAD:])
    inputs = wide(tokens_ref[...])
    inverse = inverse_rms(inputs)
    normed = inputs * inverse
    turned = low_of(normed * gains_ref[0:1, :]).T
    for at in range(0, split_qkv, tile):
        dwa[:, at : at + tile] = low_of(
            jnp.dot(turned, proj[:, at : at + tile], preferred_element_type=jnp.float32)
        )
    grad_in = nt_dot(proj[...], flat(weights[:, :, :split_qkv]))
    small[0:1, :] = jnp.sum(grad_in * normed, axis=0, keepdims=True)
    tokens_grad_ref[...] = grad_middle_ref[...] + rms_back_of(
        grad_in * gains_ref[0:1, :], normed, inverse
    )


def reduce_group_flow(copies, times, group, source, ztrans, zin, zout, yin, yout, gathered, out_ref):
    z_right, z_left, _ = ring_peers("z")
    flip, beside, _ = column_peers()
    chip_z, half = lax.axis_index("z"), lax.axis_index("h")
    part = source.shape[0] // 8

    def rows(z_step, place):
        block = lax.rem(chip_z + z_step, CHIPS) * 2 + place
        return pl.ds(pl.multiple_of(block * part, part), part)

    yield times[0]
    far_r = copies.start(source.at[rows(2, 0)], ztrans.at[0], z_right)
    far_l = copies.start(source.at[rows(2, 1)], ztrans.at[1], z_left)
    plain_r = copies.start(source.at[rows(1, 1)], zin.at[0, 1], z_right)
    plain_l = copies.start(source.at[rows(3, 0)], zin.at[1, 0], z_left)
    yield times[1]
    far_r.wait_recv()
    zout[0] = low_of(wide(source[rows(1, 0), :]) + wide(ztrans[0]))
    sum_r = copies.start(zout.at[0], zin.at[0, 0], z_right)
    far_l.wait_recv()
    zout[1] = low_of(wide(source[rows(3, 1), :]) + wide(ztrans[1]))
    sum_l = copies.start(zout.at[1], zin.at[1, 1], z_left)
    yield times[2]
    plain_r.wait_recv()
    plain_l.wait_recv()
    sum_r.wait_recv()
    sum_l.wait_recv()
    yout[0] = low_of(
        wide(source[rows(0, 1 - half), :]) + wide(zin[0, 1 - half]) + wide(zin[1, 1 - half])
    )
    over = copies.start(yout.at[0], yin.at[0], flip)
    yield times[3]
    over.wait_recv()
    own = wide(source[rows(0, half), :]) + wide(zin[0, half]) + wide(zin[1, half]) + wide(yin[0])
    yout[1] = low_of(own)
    next_to = copies.start(yout.at[1], yin.at[1], beside)
    yield from spread_group(copies, times[4:], group, next_to, yin, yout, gathered, out_ref)


def flip_group_flow(copies, times, group, source, flipped, ztrans, zin, zout, yin, yout, gathered, out_ref):
    z_right, z_left, _ = ring_peers("z")
    flip, beside, _ = column_peers()
    chip_z, half = lax.axis_index("z"), lax.axis_index("h")
    part = source.shape[0] // 8
    top, rest = pl.ds(0, SPLIT), pl.ds(SPLIT, part - SPLIT)
    short = pl.ds(0, part - SPLIT)

    def block(z_step):
        return lax.rem(chip_z + z_step, CHIPS)

    def rows(z_step, place):
        return pl.ds(pl.multiple_of((block(z_step) * 2 + place) * part, part), part)

    order = (2, 1, 3, 0)
    yield times[0]
    over = [
        copies.start(source.at[rows(step, 1 - half)], flipped.at[block(step)], flip) for step in order
    ]
    yield times[1]
    for step, copy in zip(order, over):
        copy.wait_recv()
        flipped[block(step)] = low_of(
            wide(source[rows(step, half), :]) + wide(flipped[block(step)])
        )
    far_r = copies.start(flipped.at[block(2), top], ztrans.at[0, top], z_right)
    far_l = copies.start(flipped.at[block(2), rest], ztrans.at[1, short], z_left)
    plain_r = copies.start(flipped.at[block(1), rest], zin.at[0, 0, rest], z_right)
    plain_l = copies.start(flipped.at[block(3), top], zin.at[1, 0, top], z_left)
    yield times[2]
    far_r.wait_recv()
    zout[0, top, :] = low_of(wide(flipped[block(1), top, :]) + wide(ztrans[0, top, :]))
    sum_r = copies.start(zout.at[0, top], zin.at[0, 0, top], z_right)
    far_l.wait_recv()
    zout[1, short, :] = low_of(wide(flipped[block(3), rest, :]) + wide(ztrans[1, short, :]))
    sum_l = copies.start(zout.at[1, short], zin.at[1, 0, rest], z_left)
    yield times[3]
    for copy in (plain_r, plain_l, sum_r, sum_l):
        copy.wait_recv()
    yout[1] = low_of(wide(flipped[block(0)]) + wide(zin[0, 0]) + wide(zin[1, 0]))
    next_to = copies.start(yout.at[1], yin.at[1], beside)
    yield from spread_group(copies, times[4:], group, next_to, yin, yout, gathered, out_ref)


def spread_group(copies, times, group, next_to, yin, yout, gathered, out_ref):
    x_right, x_left, _ = ring_peers("x")
    chip_x, core = lax.axis_index("x"), lax.axis_index("c")
    sibling = {"c": 1 - core}
    part = yout.shape[1]
    yield times[0]
    next_to.wait_recv()

    def slot(x_step, of_core):
        return lax.rem(chip_x + x_step, CHIPS) * 2 + of_core

    mine = slot(0, core)
    split = 80
    gathered[mine] = low_of(wide(yout[1]) + wide(yin[1]))
    from_left = copies.start(gathered.at[mine], gathered.at[mine], x_right)
    from_right = copies.start(gathered.at[mine], gathered.at[mine], x_left)
    shared = [copies.start(gathered.at[mine], gathered.at[mine], sibling)]
    yield times[1]
    from_left.wait_recv()
    seen = slot(3, core)
    far_first = copies.start(
        gathered.at[seen, pl.ds(0, split)], gathered.at[seen, pl.ds(0, split)], x_right
    )
    shared.append(copies.start(gathered.at[seen], gathered.at[seen], sibling))
    from_right.wait_recv()
    seen = slot(1, core)
    rest = pl.ds(split, part - split)
    far_second = copies.start(gathered.at[seen, rest], gathered.at[seen, rest], x_left)
    shared.append(copies.start(gathered.at[seen], gathered.at[seen], sibling))
    yield times[2]
    far_first.wait_recv()
    far_second.wait_recv()
    seen = slot(2, core)
    shared.append(copies.start(gathered.at[seen], gathered.at[seen], sibling))
    yield times[3]
    for copy in shared:
        copy.wait_recv()
    width = yout.shape[2]
    own_rows = part // 2
    for place in range(8):
        values = wide(gathered[place])
        picked = low_of(jnp.where(core == 0, values[:own_rows], values[own_rows:]))
        for tile in range(0, width, LANES):
            if group == 2:
                which, at = 2, place * width + tile
            else:
                number = (group * width + tile) // LANES
                which, at = number % 2, place * width + number // 2 * LANES
            if at < FF:
                first = which * FF + at
                out_ref[:, first : first + LANES] = picked[:, tile : tile + LANES]


def reduce_attn_flow(copies, times, source, base, cin, xtrans, xin, xout, zin, zown, yin, yown, gathered, other, out_ref):
    x_peers, z_peers, y_peers = ring_peers("x"), ring_peers("z"), column_peers()
    chip_x, chip_z, core, half = (
        lax.axis_index("x"),
        lax.axis_index("z"),
        lax.axis_index("c"),
        lax.axis_index("h"),
    )
    sibling = {"c": 1 - core}
    part, width = source.shape[0] // 8, cin.shape[2]
    cols = width // CHIPS
    span = pl.ds(base, width)

    def rows(block, place):
        return pl.ds(pl.multiple_of((block * 2 + place) * part, part), part)

    def columns(x_step):
        return pl.ds(pl.multiple_of(lax.rem(chip_x + x_step, CHIPS) * cols, cols), cols)

    yield times[0]
    given = [
        copies.start(source.at[rows(b, 1 - core), span], cin.at[b], sibling) for b in range(4)
    ]
    yield times[1]
    for b in range(4):
        given[b].wait_recv()
        cin[b] = low_of(wide(source[rows(b, core), span]) + wide(cin[b]))
    front, back = pl.ds(0, 2), pl.ds(2, 2)
    far_r = copies.start(cin.at[front, :, columns(2)], xtrans.at[0], x_peers[0])
    far_l = copies.start(cin.at[back, :, columns(2)], xtrans.at[1], x_peers[1])
    plain_r = copies.start(cin.at[back, :, columns(1)], xin.at[0, back], x_peers[0])
    plain_l = copies.start(cin.at[front, :, columns(3)], xin.at[1, front], x_peers[1])
    yield times[2]
    far_r.wait_recv()
    xout[0] = low_of(wide(cin[front, :, columns(1)]) + wide(xtrans[0]))
    sum_r = copies.start(xout.at[0], xin.at[0, front], x_peers[0])
    far_l.wait_recv()
    xout[1] = low_of(wide(cin[back, :, columns(3)]) + wide(xtrans[1]))
    sum_l = copies.start(xout.at[1], xin.at[1, back], x_peers[1])
    yield times[3]
    for copy in (plain_r, plain_l, sum_r, sum_l):
        copy.wait_recv()
    zown[...] = low_of(wide(cin[:, :, columns(0)]) + wide(xin[0]) + wide(xin[1]))
    spread = [
        copies.start(zown.at[lax.rem(chip_z + step, CHIPS)], zin.at[place], z_peers[place])
        for place, step in ((0, 1), (1, 3), (2, 2))
    ]
    yield times[4]
    for copy in spread:
        copy.wait_recv()
    yown[...] = low_of(wide(zown[chip_z]) + wide(zin[0]) + wide(zin[1]) + wide(zin[2]))
    spread = [copies.start(yown, yin.at[place], y_peers[place]) for place in range(3)]
    yield times[5]
    for copy in spread:
        copy.wait_recv()
    gathered[chip_x] = low_of(wide(yown[...]) + wide(yin[0]) + wide(yin[1]) + wide(yin[2]))
    spread = [
        copies.start(gathered.at[chip_x], gathered.at[chip_x], x_peers[place]) for place in range(3)
    ]
    yield times[6]
    for copy in spread:
        copy.wait_recv()
    crossing = copies.start(gathered, other, sibling)
    yield times[7]
    crossing.wait_recv()
    own_rows = part // 2
    for place in range(CHIPS):
        values = jnp.where(half == core, wide(gathered[place]), wide(other[place]))
        out_ref[:, base + place * cols : base + (place + 1) * cols] = low_of(
            jnp.where(core == 0, values[:own_rows], values[own_rows:])
        )


def reduce_small_flow(copies, begin, source, cin, held, xin, yin, zin, out_ref):
    core = lax.axis_index("c")
    yield begin
    crossing = copies.start(source, cin, {"c": 1 - core})
    yield begin + 5
    crossing.wait_recv()
    held[0] = source[...] + cin[...]
    for number, (peers, inbox) in enumerate(
        ((ring_peers("x"), xin), (ring_peers("z"), zin), (column_peers(), yin))
    ):
        spread = [copies.start(held.at[number], inbox.at[place], peers[place]) for place in range(3)]
        yield begin + 9 + 4 * number
        for copy in spread:
            copy.wait_recv()
        total = held[number] + inbox[0] + inbox[1] + inbox[2]
        if number < 2:
            held[number + 1] = total
        else:
            out_ref[...] = total


def reduce_kernel(
    gu_ref, down_ref, grad_hidden_ref, po_ref, cot_ref, tokens_ref, weights, cos_ref, sin_ref,
    gains_ref, qk_ref, raw, q_low, kv_all, probs, mixed, branch_ref, middle_ref,
    mlp_out, attn_out, small_out, tokens_grad_ref,
    ztrans, zin, zout, yin, yout, gathered, flipped,
    o_cin, o_xtrans, o_xin, o_xout, o_zin, o_zown, o_yin, o_yown, o_gathered, o_other,
    a_cin, a_xtrans, a_xin, a_xout, a_zin, a_zown, a_yin, a_yown, a_gathered, a_other,
    s_cin, s_held, s_xin, s_yin, s_zin,
    dwa, s_source, grad_kv, kv_out, kv_in, grad_q, grad_middle_ref, proj,
    mlp_sends, mlp_recvs, attn_sends, attn_recvs, small_sends, small_recvs, kv_sends, kv_recvs,
):
    core = lax.axis_index("c")
    a_buffers = (
        (o_cin, o_xtrans, o_xin, o_xout, o_zin, o_zown, o_yin, o_yown, o_gathered, o_other),
        (a_cin, a_xtrans, a_xin, a_xout, a_zin, a_zown, a_yin, a_yown, a_gathered, a_other),
    )
    meet(
        ({"c": 1 - core},) + ring_peers("x") + ring_peers("z") + column_peers()
        + tuple(block_peer(step) for step in range(-REACH, REACH) if step)
    )
    width = down_ref.shape[1]
    sources = (
        gu_ref.at[:, pl.ds(0, width)],
        gu_ref.at[:, pl.ds(width, width)],
        down_ref,
    )
    groups = [Copies(mlp_sends.at[n], mlp_recvs.at[n]) for n in range(3)]
    attn = [Copies(attn_sends.at[n], attn_recvs.at[n]) for n in range(2)]
    small = Copies(small_sends, small_recvs)
    blocks = Copies(kv_sends, kv_recvs)
    flows = [
        attention_back_flow(
            blocks, (1, 6, 8.5, 22), grad_hidden_ref, po_ref, cot_ref, tokens_ref, weights, cos_ref, sin_ref,
            (gains_ref, qk_ref, raw, q_low, kv_all, probs, mixed, branch_ref, middle_ref),
            dwa, s_source, grad_kv, kv_out, kv_in, grad_q, grad_middle_ref, proj, tokens_grad_ref,
        ),
        reduce_small_flow(small, 29, s_source, s_cin, s_held, s_xin, s_yin, s_zin, small_out),
    ]
    split_qkv = (HEADS + 2) * HEAD
    for n, (base, times) in enumerate(
        (
            (split_qkv, (5, 8, 20, 32, 39, 46, 53, 56)),
            (0, (28.5, 34, 46, 56, 63, 70, 77, 80)),
        )
    ):
        flows.append(reduce_attn_flow(attn[n], times, dwa, base, *a_buffers[n], attn_out))
    schedule = (
        (0, 14.5, 33, 41, 49, 57, 62, 65),
        (8.4, 30, 43, 51, 59, 67, 72, 75),
        (0.2, 31, 45, 52, 60, 68, 73, 77),
    )
    for n, group in enumerate((2, 0, 1)):
        shared = (ztrans.at[n], zin.at[n], zout.at[n], yin.at[n], yout.at[n], gathered.at[n], mlp_out)
        if n < 2:
            flow = reduce_group_flow(groups[n], schedule[n], group, sources[group], *shared)
        else:
            flow = flip_group_flow(groups[n], schedule[n], group, sources[group], flipped, *shared)
        flows.append(flow)
    run_flows(flows)
    for copies in groups + attn + [small, blocks]:
        copies.finish()


def reduce_call(w_gu_grad, w_down_grad, operands):
    depth, width = w_down_grad.shape
    weights, tokens = operands[4], operands[3]
    attn_width = weights.shape[2]
    rows, model_width = tokens.shape
    part = depth // 8
    bf16, f32 = jnp.bfloat16, jnp.float32

    def buffer(*shape):
        return pltpu.VMEM(shape, bf16)

    def wide_buffer(*shape):
        return pltpu.VMEM(shape, f32)

    def attn_buffers(columns):
        cols = columns // CHIPS
        return [
            buffer(4, part, columns),
            buffer(2, 2, part, cols),
            buffer(2, 4, part, cols),
            buffer(2, 2, part, cols),
            buffer(3, part, cols),
            buffer(4, part, cols),
            buffer(3, part, cols),
            buffer(part, cols),
            buffer(CHIPS, part, cols),
            buffer(CHIPS, part, cols),
        ]

    def sems(*shape):
        return [pltpu.SemaphoreType.DMA(shape)] * 2

    return pl.pallas_call(
        reduce_kernel,
        out_shape=(
            jax.ShapeDtypeStruct((part // 2, 3 * FF), bf16),
            jax.ShapeDtypeStruct((part // 2, attn_width), bf16),
            jax.ShapeDtypeStruct((8, model_width), f32),
            jax.ShapeDtypeStruct((rows, model_width), f32),
        ),
        in_specs=[vmem_spec()] * (2 + len(operands)),
        out_specs=tuple([vmem_spec()] * 4),
        scratch_shapes=[
            buffer(3, 2, part, width),
            buffer(3, 2, 2, part, width),
            buffer(3, 2, part, width),
            buffer(3, 2, part, width),
            buffer(3, 2, part, width),
            buffer(3, 8, part, width),
            buffer(CHIPS, part, width),
        ]
        + attn_buffers(HEADS * HEAD)
        + attn_buffers((HEADS + 2) * HEAD)
        + [
            wide_buffer(8, model_width),
            wide_buffer(3, 8, model_width),
            wide_buffer(3, 8, model_width),
            wide_buffer(3, 8, model_width),
            wide_buffer(3, 8, model_width),
            buffer(depth, attn_width),
            wide_buffer(8, model_width),
            wide_buffer((REACH + 1) * rows, 2 * HEAD),
            buffer(REACH, rows, 2 * HEAD),
            buffer(REACH, rows, 2 * HEAD),
            wide_buffer(rows, HEADS * HEAD),
            wide_buffer(rows, model_width),
            buffer(rows, (HEADS + 2) * HEAD),
        ]
        + sems(3, 20) + sems(2, 20) + sems(10) + sems(REACH),
        compiler_params=pltpu.CompilerParams(
            collective_id=1, has_side_effects=True, vmem_limit_bytes=63 * 1024 * 1024
        ),
        cost_estimate=pl.CostEstimate(flops=10_000_000, bytes_accessed=20_000_000, transcendentals=0),
        name="attend_back_and_reduce",
    )(w_gu_grad, w_down_grad, *operands)


SPLIT = 80


def plane_gather_flow(copies, times, slots, windows, shared, ready):
    z_right, z_left, _ = ring_peers("z")
    flip, beside, _ = column_peers()
    chip_z, half = lax.axis_index("z"), lax.axis_index("h")
    count = slots.shape[1]
    along = windows + ([shared[0]] if shared else [])
    handed = []

    def send(step, of_half, window, peer, first=0, size=count):
        slot = lax.rem(chip_z + step, CHIPS) * 2 + of_half
        place = slots.at[slot, pl.ds(first, size), window]
        return copies.start(place, place, peer)

    def both(step, of_half):
        return [[send(step, of_half, window, peer) for window in along] for peer in (z_right, z_left)]

    def wait(group):
        for copy in group:
            copy.wait_recv()

    def hand(step, of_half):
        if shared:
            handed.append(send(step, of_half, shared[0], beside))

    def onward(arrived_left, arrived_right, of_half):
        wait(arrived_left)
        first = [send(3, of_half, window, z_right, 0, SPLIT) for window in along]
        hand(3, of_half)
        wait(arrived_right)
        second = [send(1, of_half, window, z_left, SPLIT, count - SPLIT) for window in along]
        hand(1, of_half)
        return first + second

    yield times[0]
    own_right, own_left = both(0, half)
    over = [send(0, half, window, flip) for window in along + ([shared[1]] if shared else [])]
    yield times[1]
    wait(over[: len(along)])
    flip_right, flip_left = both(0, 1 - half)
    yield times[2]
    far = onward(own_right, own_left, half)
    yield times[3]
    far += onward(flip_right, flip_left, 1 - half)
    yield times[4]
    wait(far)
    hand(2, half)
    hand(2, 1 - half)
    yield times[5]
    wait(handed)
    wait(over[len(along) :])
    ready()


def gather_kernel(
    attn_ref, mlp_ref, small_ref, tokens_ref, cos_ref, sin_ref,
    attn_out, mlp_out, gains_out, qk_out, raw, q_low, kv_all, probs, mixed, branch, middle, hidden,
    small_out, shard, a_cin, m_cin, load_sem, sends, recvs,
):
    core, chip_x = lax.axis_index("c"), lax.axis_index("x")
    chip_z, half = lax.axis_index("z"), lax.axis_index("h")
    sibling = {"c": 1 - core}
    x_right, x_left, _ = ring_peers("x")
    z_peers = ring_peers("z")
    flip, _, _ = column_peers()
    load = pltpu.make_async_copy(mlp_ref, shard.at[:, pl.ds(0, mlp_ref.shape[1])], load_sem)
    load.start()
    own_rows = attn_ref.shape[0]
    width = mlp_out.shape[2] // 3
    qkv_half = (HEADS + 2) * HEAD // 2
    out_half = HEADS * HEAD // 2
    qkv = (HEADS + 2) * HEAD
    mine = chip_z * 2 + half
    groups = [Copies(sends.at[n], recvs.at[n]) for n in range(6)]
    first_copies, out_copies, mlp_copies, small_copies, block_copies, late_copies = groups
    meet(
        (sibling, x_right, x_left) + z_peers + (flip,)
        + tuple(block_peer(step) for step in range(-REACH, REACH) if step)
    )

    def lanes(at, size):
        return pl.ds(pl.multiple_of(at, LANES), size)

    def merged(own, other):
        return jnp.where(
            core == 0,
            jnp.concatenate([own, other], axis=0),
            jnp.concatenate([other, own], axis=0),
        )

    small_out[mine * 2 + core] = small_ref[...]
    small_pair = small_copies.start(
        small_out.at[mine * 2 + core], small_out.at[mine * 2 + core], sibling
    )
    given = [
        first_copies.start(
            attn_ref.at[:, lanes((1 - core) * qkv_half, qkv_half)], a_cin.at[:, pl.ds(0, qkv_half)], sibling
        ),
        first_copies.start(
            attn_ref.at[:, lanes(qkv + (1 - core) * out_half, out_half)],
            a_cin.at[:, pl.ds(qkv_half, out_half)],
            sibling,
        ),
    ]
    for copy in given:
        copy.wait_recv()
    for base, at, start, size in (
        (core * qkv_half, 0, 0, 2 * LANES),
        (core * qkv_half, (2 + chip_x) * LANES, 0, LANES),
        (qkv + core * out_half, 0, qkv_half, out_half),
    ):
        own = wide(attn_ref[:, lanes(base + at, size)])
        other = wide(a_cin[:, lanes(start + at, size)])
        attn_out[mine, :, lanes(base + at, size)] = low_of(merged(own, other))
    direct = lanes(core * qkv_half, 2 * LANES)

    def quarter(x_step):
        place = lax.rem(chip_x + x_step, CHIPS)
        return lanes(core * qkv_half + 2 * LANES + place * LANES, LANES)

    def nothing():
        return None

    turn_of = lax.rem(half + lax.axis_index("l"), 2)

    def shared_pair(base, size):
        return (lanes(base + turn_of * size, size), lanes(base + (1 - turn_of) * size, size))

    out_windows = shared_pair(qkv + core * out_half, out_half // 2)
    unshared = 5 * LANES
    mlp_windows = shared_pair(0, unshared)

    def x_flow():
        yield 14.2
        everywhere = pl.ds(0, 8)
        own = attn_out.at[everywhere, :, quarter(0)]
        to_right = first_copies.start(own, own, x_right)
        to_left = first_copies.start(own, own, x_left)
        kept = attn_out.at[everywhere, :, direct]
        shared = [first_copies.start(kept, kept, sibling)]
        yield 23
        to_right.wait_recv()
        near = attn_out.at[pl.ds(0, 4), :, quarter(3)]
        far = [first_copies.start(near, near, x_right)]
        to_left.wait_recv()
        near = attn_out.at[pl.ds(4, 4), :, quarter(1)]
        far.append(first_copies.start(near, near, x_left))
        yield 28
        for copy in far:
            copy.wait_recv()
        rest = attn_out.at[everywhere, :, lanes(core * qkv_half + 2 * LANES, 4 * LANES)]
        shared.append(first_copies.start(rest, rest, sibling))
        yield 31
        for copy in shared:
            copy.wait_recv()

    shares = []

    def share_out():
        place = attn_out.at[pl.ds(0, 8), :, lanes(qkv + core * out_half, out_half)]
        shares.append(out_copies.start(place, place, sibling))

    def out_flow():
        yield 47.5
        for copy in shares:
            copy.wait_recv()

    def mlp_exchange():
        yield 3
        load.wait()
        shard[:, pl.ds(mlp_ref.shape[1], shard.shape[1] - mlp_ref.shape[1])] = jnp.zeros(
            (own_rows, shard.shape[1] - mlp_ref.shape[1]), shard.dtype
        )
        part = chip_x * 2
        given = [
            mlp_copies.start(
                shard.at[:, lanes(n * FF + (part + 1 - core) * width, width)], m_cin.at[n], sibling
            )
            for n in range(3)
        ]
        yield 4
        for n in range(3):
            given[n].wait_recv()
            own = wide(shard[:, lanes(n * FF + (part + core) * width, width)])
            block = low_of(merged(own, wide(m_cin[n])))
            if n == 2:
                mlp_out[mine, :, 2 * width :] = block
            else:
                for at in range(0, width, LANES):
                    here = 2 * at + n * LANES
                    mlp_out[mine, :, here : here + LANES] = block[:, at : at + LANES]

    def gains_of():
        own_width, own_qk = gains_out.shape[1] // 16, qk_out.shape[1] // 16
        gains_out[...] = jnp.concatenate(
            [small_out[place][:, :own_width] for place in range(16)], axis=1
        )
        qk_out[...] = jnp.concatenate(
            [small_out[place][4:6, :own_qk] for place in range(16)], axis=1
        )

    def small_flow():
        yield 2
        small_pair.wait_recv()
        place = small_out.at[pl.ds(mine * 2, 2)]
        over = small_copies.start(place, place, flip)
        yield 4.5
        over.wait_recv()
        place = small_out.at[pl.ds(chip_z * 4, 4)]
        spread = [small_copies.start(place, place, peer) for peer in z_peers]
        yield 8
        for copy in spread:
            copy.wait_recv()

    run_flows(
        [
            plane_gather_flow(
                first_copies, (0, 7, 8, 11, 14, 14.1), attn_out, [direct, quarter(0)], None, nothing
            ),
            x_flow(),
            small_flow(),
            plane_gather_flow(
                out_copies, (8.1, 14.5, 15, 18, 21, 29), attn_out, [], out_windows, share_out,
            ),
            mlp_exchange(),
            plane_gather_flow(
                mlp_copies, (8.2, 19, 20, 24, 30, 59), mlp_out, [], mlp_windows, nothing
            ),
            plane_gather_flow(
                late_copies, (14.3, 26, 29, 42.5, 47, 60), mlp_out,
                [pl.ds(2 * unshared, 3 * width - 2 * unshared)], None,
                nothing,
            ),
            attention_flow(
                block_copies, (31.5, 42, 48), attn_out, gains_of, tokens_ref, cos_ref, sin_ref,
                (gains_out, qk_out, raw, q_low, kv_all, probs, mixed, branch, middle, hidden),
            ),
            out_flow(),
        ]
    )
    for copies in groups:
        copies.finish()


def gather_call(w_attn, w_mlp, small, tokens, cos_table, sin_table, slice_width):
    own_rows, attn_width = w_attn.shape
    rows, model_width = tokens.shape
    bf16, f32 = jnp.bfloat16, jnp.float32
    return pl.pallas_call(
        gather_kernel,
        out_shape=(
            jax.ShapeDtypeStruct((8, 2 * own_rows, attn_width), bf16),
            jax.ShapeDtypeStruct((8, 2 * own_rows, 3 * slice_width), bf16),
            jax.ShapeDtypeStruct((8, model_width), f32),
            jax.ShapeDtypeStruct((2, HEAD), f32),
            jax.ShapeDtypeStruct((rows, (HEADS + 1) * HEAD), f32),
            jax.ShapeDtypeStruct((rows, HEADS * HEAD), bf16),
            jax.ShapeDtypeStruct((REACH + 1, rows, 2 * HEAD), bf16),
            jax.ShapeDtypeStruct((HEADS, rows, (REACH + 1) * rows), f32),
            jax.ShapeDtypeStruct((rows, HEADS * HEAD), bf16),
            jax.ShapeDtypeStruct((rows, model_width), f32),
            jax.ShapeDtypeStruct((rows, model_width), f32),
            jax.ShapeDtypeStruct((rows, model_width), bf16),
        ),
        in_specs=[vmem_spec(), pl.BlockSpec(memory_space=pl.ANY)] + [vmem_spec()] * 4,
        out_specs=tuple([vmem_spec()] * 12),
        scratch_shapes=[
            pltpu.VMEM((16,) + small.shape, f32),
            pltpu.VMEM((own_rows, 2 * FF + 8 * slice_width), bf16),
            pltpu.VMEM((own_rows, attn_width // 2), bf16),
            pltpu.VMEM((3, own_rows, slice_width), bf16),
            pltpu.SemaphoreType.DMA,
            pltpu.SemaphoreType.DMA((6, 28)),
            pltpu.SemaphoreType.DMA((6, 28)),
        ],
        compiler_params=pltpu.CompilerParams(
            collective_id=2, has_side_effects=True, vmem_limit_bytes=60 * 1024 * 1024
        ),
        cost_estimate=pl.CostEstimate(flops=10_000_000, bytes_accessed=20_000_000, transcendentals=0),
        name="gather_and_attend",
    )(w_attn, w_mlp, small, tokens, cos_table, sin_table)


def shards(tokens, w_attn, w_mlp, norm_gains, qk_gains, cotangent):
    seq_count, block_len, model_width = tokens.shape
    row_count = seq_count * block_len
    seq_index = lax.axis_index("x") * 2 + lax.axis_index("l")
    slice_width = -(-FF // (8 * LANES)) * LANES
    inputs = tokens.reshape(row_count, model_width)
    grad_out = cotangent.reshape(row_count, model_width)
    own_width, own_qk = norm_gains.shape[1], qk_gains.shape[1]
    small = jnp.concatenate(
        [
            jnp.pad(norm_gains.astype(jnp.float32), ((0, 0), (0, LANES - own_width))),
            jnp.pad(qk_gains.astype(jnp.float32), ((0, 2), (0, LANES - own_qk))),
        ],
        axis=0,
    )
    positions = (seq_index * block_len + jnp.arange(block_len, dtype=jnp.int32)).astype(jnp.float32)
    half_size = HEAD // 2
    frequency = ROPE_BASE ** (-(jnp.arange(half_size, dtype=jnp.float32) * 2.0) / HEAD)
    angles = positions[:, None] * frequency[None, :]
    tables = (jnp.cos(angles), jnp.sin(angles))
    attn_full, mlp_part, gains, qk, raw, q_low, kv_all, probs, mixed, branch, middle, hidden = (
        gather_call(w_attn, w_mlp, small, inputs, *tables, slice_width)
    )
    result, grad_hidden, gain_row, upper_part, lower_part = mlp_call(
        hidden,
        middle,
        grad_out,
        mlp_part.reshape(model_width, 3 * slice_width),
        gains[3:4],
    )
    mlp_total, attn_total, small, grad_inputs = reduce_call(
        upper_part,
        lower_part,
        (grad_hidden, gain_row, grad_out, inputs, attn_full, *tables, gains, qk, raw, q_low, kv_all)
        + (probs, mixed, branch, middle),
    )
    fsdp_index = lax.axis_index(("z", "h", "c"))
    gain_total = lax.dynamic_slice_in_dim(small[:4], fsdp_index * own_width, own_width, axis=1)
    qk_total = lax.dynamic_slice_in_dim(
        small[4, : 2 * HEAD].reshape(2, HEAD), fsdp_index * own_qk, own_qk, axis=1
    )
    return (
        result.reshape(tokens.shape),
        grad_inputs.reshape(tokens.shape),
        attn_total.astype(jnp.float32),
        mlp_total.astype(jnp.float32),
        gain_total,
        qk_total,
    )


def solution(mesh):
    fine = Mesh(mesh.devices.reshape(4, 2, 4, 2, 2), ("x", "l", "z", "h", "c"))
    fsdp = ("z", "h", "c")
    seq = ("x", "l")
    in_specs = (
        P(fsdp, seq, None),
        P(fsdp, None),
        P(fsdp, None),
        P(None, fsdp),
        P(None, fsdp),
        P(fsdp, seq, None),
    )
    out_specs = (
        P(fsdp, seq, None),
        P(fsdp, seq, None),
        P(fsdp, None),
        P(fsdp, None),
        P(None, fsdp),
        P(None, fsdp),
    )
    return jax.shard_map(shards, mesh=fine, in_specs=in_specs, out_specs=out_specs, check_vma=False)
```
